32 devices in a mesh: groups: 2 (over x), section: 16 (over z, y, core).
Axes of the slice: x: 2, y: 2, z: 4, core: 2. Of those that a mesh axis runs over, the one named last changes fastest.
Arguments:
- tiles: float32 [32, 256, 256], P(('groups', 'section')), parts along dimension 0, may hold values from -6 to 6
- partners: int32 [32, 3], P(('groups', 'section')), parts along dimension 0, may hold values from 0 to 1, as said below
Outputs:
- shifts: float32 [32, 3, 9, 1024], P(('groups', 'section')), parts along dimension 0
The draws below stay inside these ranges and needn't reach their ends.
There are 2 independent parts, one for each index of `groups`. The reference program is written for one: setup_inputs(seed, part) draws one part's arguments, and reference() takes and returns one part's arrays. A program takes and returns all parts, laid end to end along the dimension named above; each array names one. Nothing has to cross between parts.
Inputs may be any that keep to these rules, and one draw needn't show every extreme that they name: `partners`: every section lists at least one partner offset.
All inputs are finite; a program needn't handle non-finite values.
Results may differ from the reference program's by a relative error of at most 0.00007.
Values sent between devices are 32-bit elements; how exact they have to be, the bound alone decides.
A program may use at most 64 MiB of HBM per device.

```python
import jax
import jax.numpy as jnp
from jax import lax

PATCH = 128
TILE = 128
REACH = 3
CROP = 32
GRID = 3
SECTIONS = 16


def draw_partners(key, part):
    random_bits = jax.random.randint(jax.random.fold_in(key, 11), (SECTIONS, REACH), 0, 2)
    chosen = jax.random.randint(jax.random.fold_in(key, 12), (SECTIONS, 1), 0, REACH)
    forced = (jnp.arange(REACH, dtype=jnp.int32)[None, :] == chosen).astype(jnp.int32)
    return jnp.maximum(random_bits, forced).astype(jnp.int32)


def shard_levels(own_key, extent, pieces, least, high):
    factor_of = 1.0
    for axis_at, blocks in pieces:
        draws = jax.random.uniform(jax.random.fold_in(jax.random.fold_in(own_key, 6), axis_at), (blocks,), jnp.float32, least / len(pieces), high / len(pieces))
        factor_of = factor_of * jnp.repeat(jnp.exp(draws), extent[axis_at] // blocks).reshape((-1,) + (1,) * (len(extent) - 1 - axis_at))
    return factor_of


def gaussian(stream_key, extent, width, most, pieces=(), held_as=jnp.bfloat16):
    drawn = jax.random.normal(stream_key, extent, jnp.float32) * width
    if len(pieces) > 0:
        drawn = shard_levels(stream_key, extent, pieces, -0.22, 0.18) * drawn
    return jnp.clip(drawn, min=-most, max=most).astype(held_as)


def setup_inputs(seed: int = 0, part: int = 0) -> dict:
    key_list = jax.random.split(jax.random.key(seed), 3)
    own_keys = jax.random.split(jax.random.fold_in(key_list[2], part), 3)
    tiles = gaussian(own_keys[0], (SECTIONS, TILE + PATCH, TILE + PATCH), 1.0, 6.0, ((0, 16),), jnp.float32)
    partners = draw_partners(jax.random.fold_in(jax.random.fold_in(key_list[2], part), 71), part)
    return {"tiles": tiles, "partners": partners}


def cut_patches(tiles, patch):
    count = tiles.shape[0]
    stride = patch // 2
    grid = tiles.shape[-1] // stride - 1
    blocks = tiles.reshape(count, grid + 1, stride, grid + 1, stride)
    rowwise = jnp.concatenate([blocks[:, :-1], blocks[:, 1:]], axis=2)
    joined = jnp.concatenate([rowwise[:, :, :, :-1], rowwise[:, :, :, 1:]], axis=4)
    return joined.transpose(0, 1, 3, 2, 4).reshape(count, grid * grid, patch, patch)

def standardize(patches):
    middle = lax.optimization_barrier(jnp.mean(patches, axis=(-2, -1), keepdims=True))
    centred = patches - middle
    spread = jnp.sqrt(lax.optimization_barrier(jnp.mean(centred * centred, axis=(-2, -1), keepdims=True)) + 1e-06)
    return centred / spread

def reference(tiles, partners):
    kept = jnp.concatenate([jnp.arange(PATCH - CROP // 2, PATCH), jnp.arange(0, CROP // 2)]).astype(jnp.int32)

    def spectrum(tile):
        return jnp.fft.fft2(standardize(cut_patches(tile[None], PATCH))[0])
    spectra = lax.map(spectrum, tiles)
    padded = jnp.concatenate([spectra, jnp.zeros((REACH,) + spectra.shape[1:], spectra.dtype)], axis=0)

    def one_section(index):
        mine = spectra[index]
        others = lax.dynamic_slice_in_dim(padded, index + 1, REACH, 0)
        whole = jnp.real(jnp.fft.ifft2(jnp.conj(mine)[None] * others))
        block = jnp.take(jnp.take(whole, kept, axis=2), kept, axis=3)
        return (block / PATCH).reshape(REACH, GRID * GRID, CROP * CROP)
    result = lax.map(one_section, jnp.arange(SECTIONS, dtype=jnp.int32))
    where_sec = jnp.arange(SECTIONS, dtype=jnp.int32)[:, None]
    offsets = jnp.arange(REACH, dtype=jnp.int32)[None, :] + 1
    listed = (partners == 1) & (where_sec + offsets < SECTIONS)
    return jnp.where(listed[:, :, None, None], result, 0.0).astype(jnp.float32)
```

```python
import functools
import math

import jax
import jax.numpy as jnp
import ml_dtypes
import numpy as np
from jax import lax
from jax.experimental import pallas as pl
from jax.experimental.pallas import tpu as pltpu
from jax.sharding import PartitionSpec as P

PATCH = 128
REACH = 3
CROP = 32
HALF = PATCH // 2
ROWS = 80
CHUNKS = 2
BF = jnp.bfloat16


def split_table(table):
    high = table.astype(ml_dtypes.bfloat16)
    low = (table - high.astype(np.float64)).astype(ml_dtypes.bfloat16)
    return high, low


def tables():
    x = np.arange(PATCH)
    k = np.arange(ROWS)
    live = (k <= HALF)[:, None]
    turn = 2.0 * math.pi / PATCH
    angle = (k[:, None] * x[None, :] % PATCH) * turn
    column = np.concatenate([np.cos(angle) * live, np.sin(angle) * live], 0)
    high, low = split_table(column)
    first = np.concatenate(
        [np.concatenate([high, high], 1), np.concatenate([low, np.zeros_like(low)], 1)], 0
    )
    angle = (x[:, None] * x[None, :] % PATCH) * turn
    cosine, sine = np.cos(angle), np.sin(angle)
    second = np.stack(split_table(np.block([[cosine, -sine], [-sine, -cosine]])))
    kept = np.arange(CROP) - CROP // 2
    angle = (x[:, None] * np.tile(kept, PATCH // CROP)[None, :] % PATCH) * turn
    cosine, sine = np.cos(angle), np.sin(angle)
    third = np.stack(split_table(np.block([[cosine, sine], [-sine, cosine]])))
    weight = np.where(k == 0, 1.0, np.where(k < HALF, 2.0, np.where(k == HALF, 1.0, 0.0)))
    angle = (kept[:, None] * k[None, :] % PATCH) * turn
    last = np.concatenate([np.cos(angle) * weight, -np.sin(angle) * weight], 1) / float(PATCH**3)
    fourth = np.concatenate(split_table(last), 0)
    return first, second, third, fourth


def split(value):
    high = value.astype(BF)
    return high, (value - high.astype(jnp.float32)).astype(BF)


def dot(a, b):
    return jnp.dot(a, b, preferred_element_type=jnp.float32)


def kernel(total, grid, tile_ref, first, second, third, fourth, out_ref,
           slots, mine, other, seg_h, seg_l, lined, send_sem, recv_sem, forward_sem):
    me = lax.axis_index("section")
    even = lax.rem(me, 2) == 0
    odd = jnp.logical_not(even)
    piece = tile_ref.shape[0] // CHUNKS
    partner = jnp.where(even, me + 1, me - 1)

    barrier = pltpu.get_barrier_semaphore()
    writers = [
        (me + 2 < total, me + 2),
        (even & (me + 1 < total), me + 1),
        (odd & (me + 3 < total), me + 3),
        (odd & (me + 1 < total), me - 1),
    ]
    targets = [
        me >= 2,
        even & (me >= 3),
        odd,
        even & (me + 2 < total),
    ]
    for wanted, device in writers:
        @pl.when(wanted)
        def _():
            pl.semaphore_signal(barrier, inc=1, device_id={"section": device},
                                device_id_type=pl.DeviceIdType.MESH)
    pl.semaphore_wait(barrier, sum(t.astype(jnp.int32) for t in targets))

    def rows(c):
        return pl.ds(c * piece, piece)

    def send(c, slot, device, which):
        return pltpu.make_async_remote_copy(
            src_ref=tile_ref.at[rows(c)], dst_ref=slots.at[slot, rows(c)],
            send_sem=send_sem.at[which, c], recv_sem=recv_sem.at[slot, c],
            device_id={"section": device}, device_id_type=pl.DeviceIdType.MESH)

    def forward_copy(c, slot):
        return pltpu.make_async_remote_copy(
            src_ref=slots.at[1, rows(c)], dst_ref=slots.at[slot, rows(c)],
            send_sem=forward_sem.at[c], recv_sem=recv_sem.at[slot, c],
            device_id={"section": partner}, device_id_type=pl.DeviceIdType.MESH)

    def arrived(c, slot):
        pltpu.make_async_remote_copy(
            src_ref=tile_ref.at[rows(c)], dst_ref=slots.at[slot, rows(c)],
            send_sem=send_sem.at[0, c], recv_sem=recv_sem.at[slot, c],
            device_id={"section": partner}, device_id_type=pl.DeviceIdType.MESH).wait_recv()

    sends = [(me >= 2, 1, me - 2, 0), (even & (me >= 3), 2, me - 3, 1), (odd, 0, me - 1, 1)]
    for c in range(CHUNKS):
        for wanted, slot, device, which in sends:
            @pl.when(wanted)
            def _():
                send(c, slot, device, which).start()

    def transform(read, into):
        for i in range(grid):
            highs, lows = [], []
            for j in range(grid):
                block = read(pl.ds(i * HALF, PATCH), pl.ds(j * HALF, PATCH))
                middle = jnp.sum(jnp.sum(block, 0, keepdims=True), 1, keepdims=True) * (1.0 / PATCH**2)
                centred = block - middle
                spread = jnp.sum(jnp.sum(centred * centred, 0, keepdims=True), 1, keepdims=True)
                scale = 1.0 / jnp.sqrt(spread * (1.0 / PATCH**2) + 1e-06)
                high, low = split(centred * scale)
                highs.append(high)
                lows.append(low)
            stacked = jnp.concatenate(
                [jnp.concatenate(highs, 1), jnp.concatenate(lows, 1)], 0)
            seg = dot(first[...], stacked)
            seg = seg[:2 * ROWS] + seg[2 * ROWS:]
            for j in range(grid):
                at = pl.ds((i * grid + j) * ROWS, ROWS)
                part = seg[:, j * PATCH:(j + 1) * PATCH]
                high, low = split(jnp.concatenate([part[:ROWS], part[ROWS:]], 1))
                seg_h[at] = high
                seg_l[at] = low
        high = seg_h[...]
        into[...] = dot(high, second[0]) + dot(seg_l[...], second[0]) + dot(high, second[1])

    def correlate(slot):
        a_r, a_i = mine[:, :PATCH], mine[:, PATCH:]
        b_r, b_i = other[:, :PATCH], other[:, PATCH:]
        high, low = split(jnp.concatenate([a_r * b_r + a_i * b_i, a_r * b_i - a_i * b_r], 1))
        half = dot(high, third[0]) + dot(low, third[0]) + dot(high, third[1])
        highs, lows = [], []
        for p in range(grid * grid):
            part = half[p * ROWS:(p + 1) * ROWS]
            high, low = split(jnp.concatenate([part[:, :PATCH], part[:, PATCH:]], 0))
            highs.append(high)
            lows.append(low)
        table = fourth[...]
        done = dot(table, jnp.concatenate(highs, 1))
        done = done[:CROP] + done[CROP:] + dot(table[:CROP], jnp.concatenate(lows, 1))
        for p in range(grid * grid):
            lined[pl.ds(p * CROP, CROP)] = done[:, p * PATCH:(p + 1) * PATCH]
        lane = lax.broadcasted_iota(jnp.int32, (grid * grid, PATCH), 1) // CROP
        per = PATCH // CROP
        for g in range(CROP // per):
            line = lined[pl.ds(g * per, grid * grid, stride=CROP)]
            for q in range(1, per):
                line = jnp.where(lane == q, lined[pl.ds(g * per + q, grid * grid, stride=CROP)], line)
            out_ref[slot, :, g * PATCH:(g + 1) * PATCH] = line

    transform(lambda r, c: tile_ref[r, c], mine)

    def receive(slot):
        for c in range(CHUNKS):
            arrived(c, slot)

    def work(slot):
        transform(lambda r, c: slots[slot, r, c], other)
        correlate(slot)

    @pl.when(even & (me + 1 < total))
    def _():
        receive(0)

    @pl.when(even & (me + 2 < total))
    def _():
        for c in range(CHUNKS):
            arrived(c, 1)
            forward_copy(c, 0).start()

    @pl.when(odd & (me + 2 < total))
    def _():
        for c in range(CHUNKS):
            arrived(c, 1)
            forward_copy(c, 2).start()

    @pl.when(odd & (me + 1 < total))
    def _():
        receive(0)

    for slot in range(REACH):
        @pl.when(me + slot + 1 < total)
        def _():
            if slot == 2:
                receive(2)
            work(slot)

        @pl.when(me + slot + 1 >= total)
        def _():
            out_ref[slot] = jnp.zeros(out_ref.shape[1:], jnp.float32)

    for c in range(CHUNKS):
        for wanted, slot, device, which in sends:
            @pl.when(wanted)
            def _():
                send(c, slot, device, which).wait_send()

        @pl.when(me + 2 < total)
        def _():
            forward_copy(c, 0).wait_send()


def body(tiles, partners):
    side = tiles.shape[-1]
    grid = side // HALF - 1
    total = lax.axis_size("section")
    count = grid * grid
    vmem = pl.BlockSpec(memory_space=pltpu.VMEM)
    result = pl.pallas_call(
        functools.partial(kernel, total, grid),
        out_shape=jax.ShapeDtypeStruct((REACH, count, CROP * CROP), jnp.float32),
        in_specs=[vmem] * 5,
        out_specs=vmem,
        scratch_shapes=[
            pltpu.VMEM((REACH, side, side), jnp.float32),
            pltpu.VMEM((count * ROWS, 2 * PATCH), jnp.float32),
            pltpu.VMEM((count * ROWS, 2 * PATCH), jnp.float32),
            pltpu.VMEM((count * ROWS, 2 * PATCH), BF),
            pltpu.VMEM((count * ROWS, 2 * PATCH), BF),
            pltpu.VMEM((count * CROP, PATCH), jnp.float32),
            pltpu.SemaphoreType.DMA((2, CHUNKS)),
            pltpu.SemaphoreType.DMA((REACH, CHUNKS)),
            pltpu.SemaphoreType.DMA((CHUNKS,)),
        ],
        compiler_params=pltpu.CompilerParams(
            collective_id=0, has_side_effects=True, vmem_limit_bytes=48 * 1024 * 1024
        ),
    )(tiles[0], *[jnp.asarray(t) for t in tables()])
    position = lax.axis_index("section")
    offsets = jnp.arange(REACH, dtype=jnp.int32) + 1
    listed = (partners[0] == 1) & (position + offsets < total)
    return jnp.where(listed[:, None, None], result, 0.0)[None]


def solution(mesh):
    in_specs = (P(("groups", "section"), None, None), P(("groups", "section"), None))
    out_specs = P(("groups", "section"), None, None, None)
    return jax.shard_map(body, mesh=mesh, in_specs=in_specs, out_specs=out_specs, check_vma=False)
```

```python
import functools
import math

import jax
import jax.numpy as jnp
import ml_dtypes
import numpy as np
from jax import lax
from jax.experimental import pallas as pl
from jax.experimental.pallas import tpu as pltpu
from jax.sharding import PartitionSpec as P

PATCH = 128
REACH = 3
CROP = 32
HALF = PATCH // 2
ROWS = 80
CHUNKS = 2
BF = jnp.bfloat16


def split_table(table):
    high = table.astype(ml_dtypes.bfloat16)
    low = (table - high.astype(np.float64)).astype(ml_dtypes.bfloat16)
    return high, low


def thrice(table):
    high, low = split_table(table)
    return np.concatenate([high, high, low], 0)


def tables():
    x = np.arange(PATCH)
    k = np.arange(ROWS)
    live = (k <= HALF)[:, None]
    turn = 2.0 * math.pi / PATCH
    angle = (k[:, None] * x[None, :] % PATCH) * turn
    column = np.concatenate([np.cos(angle) * live, np.sin(angle) * live], 0)
    high, low = split_table(column)
    first = np.concatenate(
        [np.concatenate([high, high], 1), np.concatenate([low, np.zeros_like(low)], 1)], 0
    )
    angle = (x[:, None] * x[None, :] % PATCH) * turn
    cosine, sine = np.cos(angle), np.sin(angle)
    second = thrice(np.block([[cosine, -sine], [-sine, -cosine]]))
    kept = np.arange(CROP) - CROP // 2
    angle = (x[:, None] * np.tile(kept, PATCH // CROP)[None, :] % PATCH) * turn
    cosine, sine = np.cos(angle), np.sin(angle)
    third = thrice(np.block([[cosine, sine], [-sine, cosine]]))
    weight = np.where(k == 0, 1.0, np.where(k < HALF, 2.0, np.where(k == HALF, 1.0, 0.0)))
    angle = (kept[:, None] * k[None, :] % PATCH) * turn
    last = np.concatenate([np.cos(angle) * weight, -np.sin(angle) * weight], 1) / float(PATCH**3)
    fourth = np.concatenate(split_table(last), 0)
    return first, second, third, fourth


def split(value):
    high = value.astype(BF)
    return high, (value - high.astype(jnp.float32)).astype(BF)


def dot(a, b):
    return jnp.dot(a, b, preferred_element_type=jnp.float32)


def kernel(total, grid, tile_ref, partners_ref, first_ref, second_ref, third_ref, fourth_ref, out_ref,
           own, partners, first, second, third, fourth, load_sem, slots, mine, other, seg_h, seg_l, lined, send_sem, recv_sem, forward_sem):
    me = lax.axis_index("section")
    even = lax.rem(me, 2) == 0
    odd = jnp.logical_not(even)
    piece = tile_ref.shape[0] // CHUNKS
    partner = jnp.where(even, me + 1, me - 1)
    lines = out_ref.shape[0] // REACH

    loads = [
        pltpu.make_async_copy(source, into, load_sem.at[n])
        for n, (source, into) in enumerate([
            (tile_ref, own), (first_ref, first), (second_ref, second),
            (third_ref, third), (fourth_ref, fourth), (partners_ref, partners)])
    ]
    for load in loads:
        load.start()

    barrier = pltpu.get_barrier_semaphore()
    writers = [
        (me + 2 < total, me + 2),
        (even & (me + 1 < total), me + 1),
        (odd & (me + 3 < total), me + 3),
        (odd & (me + 1 < total), me - 1),
    ]
    targets = [
        me >= 2,
        even & (me >= 3),
        odd,
        even & (me + 2 < total),
    ]
    for wanted, device in writers:
        @pl.when(wanted)
        def _():
            pl.semaphore_signal(barrier, inc=1, device_id={"section": device},
                                device_id_type=pl.DeviceIdType.MESH)
    pl.semaphore_wait(barrier, sum(t.astype(jnp.int32) for t in targets))

    def rows(c):
        return pl.ds(c * piece, piece)

    def send(c, slot, device, which):
        return pltpu.make_async_remote_copy(
            src_ref=tile_ref.at[rows(c)], dst_ref=slots.at[slot, rows(c)],
            send_sem=send_sem.at[which, c], recv_sem=recv_sem.at[slot, c],
            device_id={"section": device}, device_id_type=pl.DeviceIdType.MESH)

    def forward_copy(c, slot):
        return pltpu.make_async_remote_copy(
            src_ref=slots.at[1, rows(c)], dst_ref=slots.at[slot, rows(c)],
            send_sem=forward_sem.at[c], recv_sem=recv_sem.at[slot, c],
            device_id={"section": partner}, device_id_type=pl.DeviceIdType.MESH)

    def arrived(c, slot):
        pltpu.make_async_remote_copy(
            src_ref=tile_ref.at[rows(c)], dst_ref=slots.at[slot, rows(c)],
            send_sem=send_sem.at[0, c], recv_sem=recv_sem.at[slot, c],
            device_id={"section": partner}, device_id_type=pl.DeviceIdType.MESH).wait_recv()

    sends = [(me >= 2, 1, me - 2, 0), (even & (me >= 3), 2, me - 3, 1), (odd, 0, me - 1, 1)]
    for c in range(CHUNKS):
        for wanted, slot, device, which in sends:
            @pl.when(wanted)
            def _():
                send(c, slot, device, which).start()

    def transform(read, into):
        for i in range(grid):
            highs, lows = [], []
            for j in range(grid):
                block = read(pl.ds(i * HALF, PATCH), pl.ds(j * HALF, PATCH))
                middle = jnp.sum(jnp.sum(block, 0, keepdims=True), 1, keepdims=True) * (1.0 / PATCH**2)
                centred = block - middle
                spread = jnp.sum(jnp.sum(centred * centred, 0, keepdims=True), 1, keepdims=True)
                scale = 1.0 / jnp.sqrt(spread * (1.0 / PATCH**2) + 1e-06)
                high, low = split(centred * scale)
                highs.append(high)
                lows.append(low)
            stacked = jnp.concatenate(
                [jnp.concatenate(highs, 1), jnp.concatenate(lows, 1)], 0)
            seg = dot(first[...], stacked)
            seg = seg[:2 * ROWS] + seg[2 * ROWS:]
            for j in range(grid):
                at = pl.ds((i * grid + j) * ROWS, ROWS)
                part = seg[:, j * PATCH:(j + 1) * PATCH]
                high, low = split(jnp.concatenate([part[:ROWS], part[ROWS:]], 1))
                seg_h[at] = high
                seg_l[at] = low
        high = seg_h[...]
        into[...] = dot(jnp.concatenate([high, seg_l[...], high], 1), second[...])

    def correlate(slot):
        a_r, a_i = mine[:, :PATCH], mine[:, PATCH:]
        b_r, b_i = other[:, :PATCH], other[:, PATCH:]
        high, low = split(jnp.concatenate([a_r * b_r + a_i * b_i, a_r * b_i - a_i * b_r], 1))
        half = dot(jnp.concatenate([high, low, high], 1), third[...])
        highs, lows = [], []
        for p in range(grid * grid):
            part = half[p * ROWS:(p + 1) * ROWS]
            high, low = split(jnp.concatenate([part[:, :PATCH], part[:, PATCH:]], 0))
            highs.append(high)
            lows.append(low)
        table = fourth[...]
        done = dot(table, jnp.concatenate(highs, 1))
        done = done[:CROP] + done[CROP:] + dot(table[:CROP], jnp.concatenate(lows, 1))
        for p in range(grid * grid):
            lined[pl.ds(p * CROP, CROP)] = done[:, p * PATCH:(p + 1) * PATCH]
        lane = lax.broadcasted_iota(jnp.int32, (grid * grid, PATCH), 1) // CROP
        per = PATCH // CROP
        listed = partners[0, slot] == 1
        for g in range(CROP // per):
            line = lined[pl.ds(g * per, grid * grid, stride=CROP)]
            for q in range(1, per):
                line = jnp.where(lane == q, lined[pl.ds(g * per + q, grid * grid, stride=CROP)], line)
            out_ref[pl.ds(slot * lines + g, grid * grid, stride=CROP // per)] = jnp.where(listed, line, 0.0)

    loads[0].wait()
    loads[1].wait()
    loads[2].wait()
    transform(lambda r, c: own[r, c], mine)
    loads[3].wait()
    loads[4].wait()
    loads[5].wait()

    for step in range(REACH):
        slot = jnp.where(even, step, REACH - 1 - step)
        here = me + slot + 1 < total

        @pl.when(here)
        def _():
            for c in range(CHUNKS):
                arrived(c, slot)
                if step == 1:
                    forward_copy(c, jnp.where(even, 0, 2)).start()
            transform(lambda r, c: slots[slot, r, c], other)
            correlate(slot)

        @pl.when(jnp.logical_not(here))
        def _():
            out_ref[pl.ds(slot * lines, lines)] = jnp.zeros((lines, PATCH), jnp.float32)

    for c in range(CHUNKS):
        for wanted, slot, device, which in sends:
            @pl.when(wanted)
            def _():
                send(c, slot, device, which).wait_send()

        @pl.when(me + 2 < total)
        def _():
            forward_copy(c, 0).wait_send()


def body(tiles, partners):
    side = tiles.shape[-1]
    grid = side // HALF - 1
    total = lax.axis_size("section")
    count = grid * grid
    lines = count * CROP * CROP // PATCH
    constants = tables()
    vmem = pl.BlockSpec(memory_space=pltpu.VMEM)
    result = pl.pallas_call(
        functools.partial(kernel, total, grid),
        out_shape=jax.ShapeDtypeStruct((REACH * lines, PATCH), jnp.float32),
        in_specs=[pl.BlockSpec(memory_space=pltpu.HBM)] * 6,
        out_specs=vmem,
        scratch_shapes=[
            pltpu.VMEM((side, side), jnp.float32),
            pltpu.SMEM((1, REACH), jnp.int32),
            *[pltpu.VMEM(t.shape, BF) for t in constants],
            pltpu.SemaphoreType.DMA((6,)),
            pltpu.VMEM((REACH, side, side), jnp.float32),
            pltpu.VMEM((count * ROWS, 2 * PATCH), jnp.float32),
            pltpu.VMEM((count * ROWS, 2 * PATCH), jnp.float32),
            pltpu.VMEM((count * ROWS, 2 * PATCH), BF),
            pltpu.VMEM((count * ROWS, 2 * PATCH), BF),
            pltpu.VMEM((count * CROP, PATCH), jnp.float32),
            pltpu.SemaphoreType.DMA((2, CHUNKS)),
            pltpu.SemaphoreType.DMA((REACH, CHUNKS)),
            pltpu.SemaphoreType.DMA((CHUNKS,)),
        ],
        compiler_params=pltpu.CompilerParams(
            collective_id=0, has_side_effects=True, vmem_limit_bytes=63_000_000
        ),
    )(tiles[0], partners, *[jnp.asarray(t) for t in constants])
    return result.reshape(1, REACH, count, CROP * CROP)


def solution(mesh):
    in_specs = (P(("groups", "section"), None, None), P(("groups", "section"), None))
    out_specs = P(("groups", "section"), None, None, None)
    return jax.shard_map(body, mesh=mesh, in_specs=in_specs, out_specs=out_specs, check_vma=False)
```

```python
import functools
import math

import jax
import jax.numpy as jnp
import ml_dtypes
import numpy as np
from jax import lax
from jax.experimental import pallas as pl
from jax.experimental.pallas import tpu as pltpu
from jax.sharding import PartitionSpec as P

PATCH = 128
REACH = 3
CROP = 32
HALF = PATCH // 2
ROWS = 80
CHUNKS = 2
BF = jnp.bfloat16


def split_table(table):
    high = table.astype(ml_dtypes.bfloat16)
    low = (table - high.astype(np.float64)).astype(ml_dtypes.bfloat16)
    return high, low


def thrice(table):
    high, low = split_table(table)
    return np.concatenate([high, high, low], 0)


def tables():
    x = np.arange(PATCH)
    k = np.arange(ROWS)
    live = (k <= HALF)[:, None]
    turn = 2.0 * math.pi / PATCH
    angle = (k[:, None] * x[None, :] % PATCH) * turn
    column = np.concatenate([np.cos(angle) * live, np.sin(angle) * live], 0)
    high, low = split_table(column)
    first = np.concatenate(
        [np.concatenate([high, high], 1), np.concatenate([low, np.zeros_like(low)], 1)], 0
    )
    angle = (x[:, None] * x[None, :] % PATCH) * turn
    cosine, sine = np.cos(angle), np.sin(angle)
    second = thrice(np.block([[cosine, -sine], [-sine, -cosine]]))
    kept = np.arange(CROP) - CROP // 2
    angle = (x[:, None] * np.tile(kept, PATCH // CROP)[None, :] % PATCH) * turn
    cosine, sine = np.cos(angle), np.sin(angle)
    third = thrice(np.block([[cosine, sine], [-sine, cosine]]))
    weight = np.where(k == 0, 1.0, np.where(k < HALF, 2.0, np.where(k == HALF, 1.0, 0.0)))
    angle = (kept[:, None] * k[None, :] % PATCH) * turn
    last = np.concatenate([np.cos(angle) * weight, -np.sin(angle) * weight], 1) / float(PATCH**2)
    fourth = np.concatenate(split_table(last), 0)
    return first, second, third, fourth


def split(value):
    high = value.astype(BF)
    return high, (value - high.astype(jnp.float32)).astype(BF)


def dot(a, b):
    return jnp.dot(a, b, preferred_element_type=jnp.float32)


def kernel(total, grid, tile_ref, partners_ref, first_ref, second_ref, third_ref, fourth_ref, out_ref,
           partners, first, second, third, fourth, load_sem, slots, spectra, seg_h, seg_l, lined, send_sem, recv_sem, forward_sem):
    me = lax.axis_index("section")
    even = lax.rem(me, 2) == 0
    odd = jnp.logical_not(even)
    piece = tile_ref.shape[0] // CHUNKS
    partner = jnp.where(even, me + 1, me - 1)
    lines = out_ref.shape[0] // REACH

    loads = [
        pltpu.make_async_copy(source, into, load_sem.at[n])
        for n, (source, into) in enumerate([
            (tile_ref, slots.at[REACH]), (first_ref, first), (second_ref, second),
            (third_ref, third), (fourth_ref, fourth), (partners_ref, partners)])
    ]
    for load in loads:
        load.start()

    barrier = pltpu.get_barrier_semaphore()
    writers = [
        (me + 2 < total, me + 2),
        (even & (me + 1 < total), me + 1),
        (odd & (me + 3 < total), me + 3),
        (odd & (me + 1 < total), me - 1),
    ]
    targets = [
        me >= 2,
        even & (me >= 3),
        odd,
        even & (me + 2 < total),
    ]
    for wanted, device in writers:
        @pl.when(wanted)
        def _():
            pl.semaphore_signal(barrier, inc=1, device_id={"section": device},
                                device_id_type=pl.DeviceIdType.MESH)
    pl.semaphore_wait(barrier, sum(t.astype(jnp.int32) for t in targets))

    def rows(c):
        return pl.ds(c * piece, piece)

    def send(c, slot, device, which):
        return pltpu.make_async_remote_copy(
            src_ref=tile_ref.at[rows(c)], dst_ref=slots.at[slot, rows(c)],
            send_sem=send_sem.at[which, c], recv_sem=recv_sem.at[slot, c],
            device_id={"section": device}, device_id_type=pl.DeviceIdType.MESH)

    def forward_copy(c, slot):
        return pltpu.make_async_remote_copy(
            src_ref=slots.at[1, rows(c)], dst_ref=slots.at[slot, rows(c)],
            send_sem=forward_sem.at[c], recv_sem=recv_sem.at[slot, c],
            device_id={"section": partner}, device_id_type=pl.DeviceIdType.MESH)

    def arrived(c, slot):
        pltpu.make_async_remote_copy(
            src_ref=tile_ref.at[rows(c)], dst_ref=slots.at[slot, rows(c)],
            send_sem=send_sem.at[0, c], recv_sem=recv_sem.at[slot, c],
            device_id={"section": partner}, device_id_type=pl.DeviceIdType.MESH).wait_recv()

    sends = [(me >= 2, 1, me - 2, 0), (even & (me >= 3), 2, me - 3, 1), (odd, 0, me - 1, 1)]
    for c in range(CHUNKS):
        for wanted, slot, device, which in sends:
            @pl.when(wanted)
            def _():
                send(c, slot, device, which).start()

    def transform(read, into):
        for i in range(grid):
            highs, lows = [], []
            for j in range(grid):
                block = read(pl.ds(i * HALF, PATCH), pl.ds(j * HALF, PATCH))
                middle = jnp.sum(jnp.sum(block, 0, keepdims=True), 1, keepdims=True) * (1.0 / PATCH**2)
                centred = block - middle
                spread = jnp.sum(jnp.sum(centred * centred, 0, keepdims=True), 1, keepdims=True)
                scale = 1.0 / jnp.sqrt(spread * (1.0 / PATCH**2) + 1e-06)
                high, low = split(centred * scale)
                highs.append(high)
                lows.append(low)
            stacked = jnp.concatenate(
                [jnp.concatenate(highs, 1), jnp.concatenate(lows, 1)], 0)
            seg = dot(first[...], stacked)
            seg = seg[:2 * ROWS] + seg[2 * ROWS:]
            for j in range(grid):
                at = pl.ds((i * grid + j) * ROWS, ROWS)
                part = seg[:, j * PATCH:(j + 1) * PATCH]
                high, low = split(jnp.concatenate([part[:ROWS], part[ROWS:]], 1))
                seg_h[at] = high
                seg_l[at] = low
        high = seg_h[...]
        into[...] = dot(jnp.concatenate([high, seg_l[...], high], 1), second[...])

    def correlate(slot):
        a_r, a_i = spectra[0, :, :PATCH], spectra[0, :, PATCH:]
        b_r, b_i = spectra[1, :, :PATCH], spectra[1, :, PATCH:]
        high, low = split(jnp.concatenate([a_r * b_r + a_i * b_i, a_r * b_i - a_i * b_r], 1))
        half = dot(jnp.concatenate([high, low, high], 1), third[...])
        highs, lows = [], []
        for p in range(grid * grid):
            part = half[p * ROWS:(p + 1) * ROWS]
            high, low = split(jnp.concatenate([part[:, :PATCH], part[:, PATCH:]], 0))
            highs.append(high)
            lows.append(low)
        table = fourth[...]
        done = dot(table, jnp.concatenate(highs, 1))
        done = done[:CROP] + done[CROP:] + dot(table[:CROP], jnp.concatenate(lows, 1))
        for p in range(grid * grid):
            lined[pl.ds(p * CROP, CROP)] = done[:, p * PATCH:(p + 1) * PATCH]
        lane = lax.broadcasted_iota(jnp.int32, (grid * grid, PATCH), 1) // CROP
        per = PATCH // CROP
        listed = partners[0, slot] == 1
        for g in range(CROP // per):
            line = lined[pl.ds(g * per, grid * grid, stride=CROP)]
            for q in range(1, per):
                line = jnp.where(lane == q, lined[pl.ds(g * per + q, grid * grid, stride=CROP)], line)
            out_ref[pl.ds(slot * lines + g, grid * grid, stride=CROP // per)] = jnp.where(listed, line, 0.0)

    for load in loads:
        load.wait()

    def turn(step, carry):
        slot = jnp.where(step == 0, REACH, jnp.where(even, step - 1, REACH - step))
        here = (step == 0) | (me + slot + 1 < total)

        @pl.when(here & (step > 0))
        def _():
            for c in range(CHUNKS):
                arrived(c, slot)

                @pl.when(step == 2)
                def _():
                    forward_copy(c, jnp.where(even, 0, 2)).start()

        @pl.when(here)
        def _():
            transform(lambda r, c: slots[slot, r, c], spectra.at[jnp.minimum(step, 1)])

        @pl.when(here & (step > 0))
        def _():
            correlate(slot)

        @pl.when(jnp.logical_not(here))
        def _():
            out_ref[pl.ds(pl.multiple_of(slot * lines, 8), lines)] = jnp.zeros((lines, PATCH), jnp.float32)
        return carry

    lax.fori_loop(0, REACH + 1, turn, 0)

    for c in range(CHUNKS):
        for wanted, slot, device, which in sends:
            @pl.when(wanted)
            def _():
                send(c, slot, device, which).wait_send()

        @pl.when(me + 2 < total)
        def _():
            forward_copy(c, 0).wait_send()


def body(tiles, partners):
    side = tiles.shape[-1]
    grid = side // HALF - 1
    total = lax.axis_size("section")
    count = grid * grid
    lines = count * CROP * CROP // PATCH
    constants = tables()
    vmem = pl.BlockSpec(memory_space=pltpu.VMEM)
    result = pl.pallas_call(
        functools.partial(kernel, total, grid),
        out_shape=jax.ShapeDtypeStruct((REACH * lines, PATCH), jnp.float32),
        in_specs=[pl.BlockSpec(memory_space=pltpu.HBM)] * 6,
        out_specs=vmem,
        scratch_shapes=[
            pltpu.SMEM((1, REACH), jnp.int32),
            *[pltpu.VMEM(t.shape, BF) for t in constants],
            pltpu.SemaphoreType.DMA((6,)),
            pltpu.VMEM((REACH + 1, side, side), jnp.float32),
            pltpu.VMEM((2, count * ROWS, 2 * PATCH), jnp.float32),
            pltpu.VMEM((count * ROWS, 2 * PATCH), BF),
            pltpu.VMEM((count * ROWS, 2 * PATCH), BF),
            pltpu.VMEM((count * CROP, PATCH), jnp.float32),
            pltpu.SemaphoreType.DMA((2, CHUNKS)),
            pltpu.SemaphoreType.DMA((REACH, CHUNKS)),
            pltpu.SemaphoreType.DMA((CHUNKS,)),
        ],
        compiler_params=pltpu.CompilerParams(
            collective_id=0, has_side_effects=True, vmem_limit_bytes=63_000_000
        ),
    )(tiles[0], partners, *[jnp.asarray(t) for t in constants])
    result = lax.optimization_barrier(result * (1.0 / PATCH))
    return result.reshape(1, REACH, count, CROP * CROP)


def solution(mesh):
    in_specs = (P(("groups", "section"), None, None), P(("groups", "section"), None))
    out_specs = P(("groups", "section"), None, None, None)
    return jax.shard_map(body, mesh=mesh, in_specs=in_specs, out_specs=out_specs, check_vma=False)
```

```python
import functools
import math

import jax
import jax.numpy as jnp
import ml_dtypes
import numpy as np
from jax import lax
from jax.experimental import pallas as pl
from jax.experimental.pallas import tpu as pltpu
from jax.sharding import PartitionSpec as P

PATCH = 128
REACH = 3
CROP = 32
HALF = PATCH // 2
ROWS = 80
CHUNKS = 2
BF = jnp.bfloat16


def split_table(table):
    high = table.astype(ml_dtypes.bfloat16)
    low = (table - high.astype(np.float64)).astype(ml_dtypes.bfloat16)
    return high, low


def thrice(table):
    high, low = split_table(table)
    return np.concatenate([high, high, low], 0)


def tables():
    x = np.arange(PATCH)
    k = np.arange(ROWS)
    live = (k <= HALF)[:, None]
    turn = 2.0 * math.pi / PATCH
    angle = (k[:, None] * x[None, :] % PATCH) * turn
    column = np.concatenate([np.cos(angle) * live, np.sin(angle) * live], 0)
    high, low = split_table(column)
    first = np.concatenate(
        [np.concatenate([high, high], 1), np.concatenate([low, np.zeros_like(low)], 1)], 0
    )
    angle = (x[:, None] * x[None, :] % PATCH) * turn
    cosine, sine = np.cos(angle), np.sin(angle)
    second = thrice(np.block([[cosine, -sine], [-sine, -cosine]]))
    kept = np.arange(CROP) - CROP // 2
    angle = (x[:, None] * np.tile(kept, PATCH // CROP)[None, :] % PATCH) * turn
    cosine, sine = np.cos(angle), np.sin(angle)
    third = thrice(np.block([[cosine, sine], [-sine, cosine]]))
    weight = np.where(k == 0, 1.0, np.where(k < HALF, 2.0, np.where(k == HALF, 1.0, 0.0)))
    angle = (kept[:, None] * k[None, :] % PATCH) * turn
    last = np.concatenate([np.cos(angle) * weight, -np.sin(angle) * weight], 1) / float(PATCH**2)
    fourth = np.concatenate(split_table(last), 0)
    fourth = np.pad(fourth, ((0, 0), (0, first.shape[1] - fourth.shape[1])))
    return np.concatenate([first, fourth], 0), second, third


def split(value):
    high = value.astype(BF)
    return high, (value - high.astype(jnp.float32)).astype(BF)


def dot(a, b):
    return jnp.dot(a, b, preferred_element_type=jnp.float32)


def kernel(total, grid, tile_ref, partners_ref, first_ref, second_ref, third_ref, out_ref,
           partners, first, second, third, load_sem, slots, spectra, seg_h, seg_l, lined, send_sem, recv_sem, forward_sem):
    me = lax.axis_index("section")
    even = lax.rem(me, 2) == 0
    odd = jnp.logical_not(even)
    piece = tile_ref.shape[0] // CHUNKS
    partner = jnp.where(even, me + 1, me - 1)
    lines = out_ref.shape[0] // REACH

    loads = [
        pltpu.make_async_copy(source, into, load_sem.at[n])
        for n, (source, into) in enumerate([
            (tile_ref, slots.at[REACH]), (first_ref, first), (second_ref, second),
            (third_ref, third), (partners_ref, partners)])
    ]
    for load in loads:
        load.start()

    barrier = pltpu.get_barrier_semaphore()
    writers = [
        (me + 2 < total, me + 2),
        (even & (me + 1 < total), me + 1),
        (odd & (me + 3 < total), me + 3),
        (odd & (me + 1 < total), me - 1),
    ]
    targets = [
        me >= 2,
        even & (me >= 3),
        odd,
        even & (me + 2 < total),
    ]
    for wanted, device in writers:
        @pl.when(wanted)
        def _():
            pl.semaphore_signal(barrier, inc=1, device_id={"section": device},
                                device_id_type=pl.DeviceIdType.MESH)
    pl.semaphore_wait(barrier, sum(t.astype(jnp.int32) for t in targets))

    def rows(c):
        return pl.ds(c * piece, piece)

    def send(c, slot, device, which):
        return pltpu.make_async_remote_copy(
            src_ref=tile_ref.at[rows(c)], dst_ref=slots.at[slot, rows(c)],
            send_sem=send_sem.at[which, c], recv_sem=recv_sem.at[slot, c],
            device_id={"section": device}, device_id_type=pl.DeviceIdType.MESH)

    def forward_copy(c, slot):
        return pltpu.make_async_remote_copy(
            src_ref=slots.at[1, rows(c)], dst_ref=slots.at[slot, rows(c)],
            send_sem=forward_sem.at[c], recv_sem=recv_sem.at[slot, c],
            device_id={"section": partner}, device_id_type=pl.DeviceIdType.MESH)

    def arrived(c, slot):
        pltpu.make_async_remote_copy(
            src_ref=tile_ref.at[rows(c)], dst_ref=slots.at[slot, rows(c)],
            send_sem=send_sem.at[0, c], recv_sem=recv_sem.at[slot, c],
            device_id={"section": partner}, device_id_type=pl.DeviceIdType.MESH).wait_recv()

    sends = [(me >= 2, 1, me - 2, 0), (even & (me >= 3), 2, me - 3, 1), (odd, 0, me - 1, 1)]
    quick = lax.rem(me // 2, 2) == 1

    def start(which_sends):
        for c in range(CHUNKS):
            for wanted, slot, device, which in which_sends:
                @pl.when(wanted)
                def _():
                    send(c, slot, device, which).start()

    start([sends[0], sends[2], (quick & sends[1][0],) + sends[1][1:]])

    def transform(read, into):
        def block(i, j):
            return read(pl.ds(i * HALF, PATCH), pl.ds(j * HALF, PATCH))

        def mean(value):
            return jnp.sum(jnp.sum(value, 0, keepdims=True), 1, keepdims=True) * (1.0 / PATCH**2)

        places = [(i, j) for i in range(grid) for j in range(grid)]
        middles = [mean(block(i, j)) for i, j in places]
        spreads = [mean((block(i, j) - m) ** 2) for (i, j), m in zip(places, middles)]
        scales = [1.0 / jnp.sqrt(v + 1e-06) for v in spreads]
        for i in range(grid):
            highs, lows = [], []
            for j in range(grid):
                at = i * grid + j
                high, low = split((block(i, j) - middles[at]) * scales[at])
                highs.append(high)
                lows.append(low)
            stacked = jnp.concatenate(
                [jnp.concatenate(highs, 1), jnp.concatenate(lows, 1)], 0)
            seg = dot(first[:4 * ROWS], stacked)
            seg = seg[:2 * ROWS] + seg[2 * ROWS:]
            for j in range(grid):
                at = pl.ds((i * grid + j) * ROWS, ROWS)
                part = seg[:, j * PATCH:(j + 1) * PATCH]
                high, low = split(jnp.concatenate([part[:ROWS], part[ROWS:]], 1))
                seg_h[at] = high
                seg_l[at] = low
        high = seg_h[...]
        into[...] = dot(jnp.concatenate([high, seg_l[...], high], 1), second[...])

    def correlate(slot):
        a_r, a_i = spectra[0, :, :PATCH], spectra[0, :, PATCH:]
        b_r, b_i = spectra[1, :, :PATCH], spectra[1, :, PATCH:]
        high, low = split(jnp.concatenate([a_r * b_r + a_i * b_i, a_r * b_i - a_i * b_r], 1))
        half = dot(jnp.concatenate([high, low, high], 1), third[...])
        highs, lows = [], []
        for p in range(grid * grid):
            part = half[p * ROWS:(p + 1) * ROWS]
            high, low = split(jnp.concatenate([part[:, :PATCH], part[:, PATCH:]], 0))
            highs.append(high)
            lows.append(low)
        table = first[4 * ROWS:, :2 * ROWS]
        done = dot(table, jnp.concatenate(highs, 1))
        done = done[:CROP] + done[CROP:] + dot(table[:CROP], jnp.concatenate(lows, 1))
        for p in range(grid * grid):
            lined[pl.ds(p * CROP, CROP)] = done[:, p * PATCH:(p + 1) * PATCH]
        lane = lax.broadcasted_iota(jnp.int32, (grid * grid, PATCH), 1) // CROP
        per = PATCH // CROP
        listed = partners[0, slot] == 1
        for g in range(CROP // per):
            line = lined[pl.ds(g * per, grid * grid, stride=CROP)]
            for q in range(1, per):
                line = jnp.where(lane == q, lined[pl.ds(g * per + q, grid * grid, stride=CROP)], line)
            out_ref[pl.ds(slot * lines + g, grid * grid, stride=CROP // per)] = jnp.where(listed, line, 0.0)

    for load in loads:
        load.wait()

    def turn(step, carry):
        odd_slot = jnp.where(step == REACH, 0, jnp.where(quick, REACH - step, step))
        slot = jnp.where(step == 0, REACH, jnp.where(even, step - 1, odd_slot))
        here = (step == 0) | (me + slot + 1 < total)

        @pl.when(step == 2)
        def _():
            start([(jnp.logical_not(quick) & sends[1][0],) + sends[1][1:]])

        @pl.when(here & (step > 0))
        def _():
            for c in range(CHUNKS):
                arrived(c, slot)

                @pl.when(slot == 1)
                def _():
                    forward_copy(c, jnp.where(even, 0, 2)).start()

        @pl.when(here)
        def _():
            transform(lambda r, c: slots[slot, r, c], spectra.at[jnp.minimum(step, 1)])

        @pl.when(here & (step > 0))
        def _():
            correlate(slot)

        @pl.when(jnp.logical_not(here))
        def _():
            out_ref[pl.ds(pl.multiple_of(slot * lines, 8), lines)] = jnp.zeros((lines, PATCH), jnp.float32)
        return carry

    lax.fori_loop(0, REACH + 1, turn, 0)

    for c in range(CHUNKS):
        for wanted, slot, device, which in sends:
            @pl.when(wanted)
            def _():
                send(c, slot, device, which).wait_send()

        @pl.when(me + 2 < total)
        def _():
            forward_copy(c, 0).wait_send()


def body(tiles, partners):
    side = tiles.shape[-1]
    grid = side // HALF - 1
    total = lax.axis_size("section")
    count = grid * grid
    lines = count * CROP * CROP // PATCH
    constants = tables()
    vmem = pl.BlockSpec(memory_space=pltpu.VMEM)
    result = pl.pallas_call(
        functools.partial(kernel, total, grid),
        out_shape=jax.ShapeDtypeStruct((REACH * lines, PATCH), jnp.float32),
        in_specs=[pl.BlockSpec(memory_space=pltpu.HBM)] * 5,
        out_specs=vmem,
        scratch_shapes=[
            pltpu.SMEM((1, REACH), jnp.int32),
            *[pltpu.VMEM(t.shape, BF) for t in constants],
            pltpu.SemaphoreType.DMA((5,)),
            pltpu.VMEM((REACH + 1, side, side), jnp.float32),
            pltpu.VMEM((2, count * ROWS, 2 * PATCH), jnp.float32),
            pltpu.VMEM((count * ROWS, 2 * PATCH), BF),
            pltpu.VMEM((count * ROWS, 2 * PATCH), BF),
            pltpu.VMEM((count * CROP, PATCH), jnp.float32),
            pltpu.SemaphoreType.DMA((2, CHUNKS)),
            pltpu.SemaphoreType.DMA((REACH, CHUNKS)),
            pltpu.SemaphoreType.DMA((CHUNKS,)),
        ],
        compiler_params=pltpu.CompilerParams(
            collective_id=0, has_side_effects=True, vmem_limit_bytes=63_000_000
        ),
    )(tiles[0], partners, *[jnp.asarray(t) for t in constants])
    result = lax.optimization_barrier(result * (1.0 / PATCH))
    return result.reshape(1, REACH, count, CROP * CROP)


def solution(mesh):
    in_specs = (P(("groups", "section"), None, None), P(("groups", "section"), None))
    out_specs = P(("groups", "section"), None, None, None)
    return jax.shard_map(body, mesh=mesh, in_specs=in_specs, out_specs=out_specs, check_vma=False)
```

```python
import functools
import math

import jax
import jax.numpy as jnp
import ml_dtypes
import numpy as np
from jax import lax
from jax.experimental import pallas as pl
from jax.experimental.pallas import tpu as pltpu
from jax.sharding import PartitionSpec as P

PATCH = 128
REACH = 3
CROP = 32
HALF = PATCH // 2
ROWS = 80
CHUNKS = 2
BF = jnp.bfloat16


def split_table(table):
    high = table.astype(ml_dtypes.bfloat16)
    low = (table - high.astype(np.float64)).astype(ml_dtypes.bfloat16)
    return high, low


def thrice(table):
    high, low = split_table(table)
    return np.concatenate([high, high, low], 0)


def tables():
    x = np.arange(PATCH)
    k = np.arange(ROWS)
    live = (k <= HALF)[:, None]
    turn = 2.0 * math.pi / PATCH
    angle = (k[:, None] * x[None, :] % PATCH) * turn
    column = np.concatenate([np.cos(angle) * live, np.sin(angle) * live], 0)
    high, low = split_table(column)
    first = np.concatenate(
        [np.concatenate([high, high], 1), np.concatenate([low, np.zeros_like(low)], 1)], 0
    )
    angle = (x[:, None] * x[None, :] % PATCH) * turn
    cosine, sine = np.cos(angle), np.sin(angle)
    second = thrice(np.block([[cosine, -sine], [-sine, -cosine]]))
    kept = np.arange(CROP) - CROP // 2
    angle = (x[:, None] * np.tile(kept, PATCH // CROP)[None, :] % PATCH) * turn
    cosine, sine = np.cos(angle), np.sin(angle)
    third = thrice(np.block([[cosine, sine], [-sine, cosine]]))
    weight = np.where(k == 0, 1.0, np.where(k < HALF, 2.0, np.where(k == HALF, 1.0, 0.0)))
    angle = (kept[:, None] * k[None, :] % PATCH) * turn
    last = np.concatenate([np.cos(angle) * weight, -np.sin(angle) * weight], 1) / float(PATCH**2)
    fourth = np.concatenate(split_table(last), 0)
    fourth = np.pad(fourth, ((0, 0), (0, first.shape[1] - fourth.shape[1])))
    return np.concatenate([first, fourth], 0), second, third


def split(value):
    high = value.astype(BF)
    return high, (value - high.astype(jnp.float32)).astype(BF)


def dot(a, b):
    return jnp.dot(a, b, preferred_element_type=jnp.float32)


def kernel(total, grid, tile_ref, partners_ref, first_ref, second_ref, third_ref, out_ref,
           partners, first, second, third, load_sem, slots, spectra, seg_h, seg_l, lined, send_sem, recv_sem, forward_sem):
    me = lax.axis_index("section")
    even = lax.rem(me, 2) == 0
    odd = jnp.logical_not(even)
    piece = tile_ref.shape[0] // CHUNKS
    partner = jnp.where(even, me + 1, me - 1)
    lines = out_ref.shape[0] // REACH

    loads = [
        pltpu.make_async_copy(source, into, load_sem.at[n])
        for n, (source, into) in enumerate([
            (tile_ref, slots.at[REACH]), (first_ref, first), (second_ref, second),
            (third_ref, third), (partners_ref, partners)])
    ]
    for load in loads:
        load.start()

    barrier = pltpu.get_barrier_semaphore()
    writers = [
        (me + 2 < total, me + 2),
        (even & (me + 1 < total), me + 1),
        (odd & (me + 3 < total), me + 3),
        (odd & (me + 1 < total), me - 1),
    ]
    targets = [
        me >= 2,
        even & (me >= 3),
        odd,
        even & (me + 2 < total),
    ]
    for wanted, device in writers:
        @pl.when(wanted)
        def _():
            pl.semaphore_signal(barrier, inc=1, device_id={"section": device},
                                device_id_type=pl.DeviceIdType.MESH)
    pl.semaphore_wait(barrier, sum(t.astype(jnp.int32) for t in targets))

    def rows(c):
        return pl.ds(c * piece, piece)

    def send(c, slot, device, which):
        return pltpu.make_async_remote_copy(
            src_ref=tile_ref.at[rows(c)], dst_ref=slots.at[slot, rows(c)],
            send_sem=send_sem.at[which, c], recv_sem=recv_sem.at[slot, c],
            device_id={"section": device}, device_id_type=pl.DeviceIdType.MESH)

    def forward_copy(c, slot):
        return pltpu.make_async_remote_copy(
            src_ref=slots.at[1, rows(c)], dst_ref=slots.at[slot, rows(c)],
            send_sem=forward_sem.at[c], recv_sem=recv_sem.at[slot, c],
            device_id={"section": partner}, device_id_type=pl.DeviceIdType.MESH)

    def arrived(c, slot):
        pltpu.make_async_remote_copy(
            src_ref=tile_ref.at[rows(c)], dst_ref=slots.at[slot, rows(c)],
            send_sem=send_sem.at[0, c], recv_sem=recv_sem.at[slot, c],
            device_id={"section": partner}, device_id_type=pl.DeviceIdType.MESH).wait_recv()

    sends = [(me >= 2, 1, me - 2, 0), (even & (me >= 3), 2, me - 3, 1), (odd, 0, me - 1, 1)]
    quick = lax.rem(me // 2, 2) == 1

    def start(which_sends):
        for c in range(CHUNKS):
            for wanted, slot, device, which in which_sends:
                @pl.when(wanted)
                def _():
                    send(c, slot, device, which).start()

    start([(even & sends[0][0],) + sends[0][1:], sends[2], (quick & sends[1][0],) + sends[1][1:]])

    def transform(read, into):
        def block(i, j):
            return read(pl.ds(i * HALF, PATCH), pl.ds(j * HALF, PATCH))

        def mean(value):
            return jnp.sum(jnp.sum(value, 0, keepdims=True), 1, keepdims=True) * (1.0 / PATCH**2)

        places = [(i, j) for i in range(grid) for j in range(grid)]
        middles = [mean(block(i, j)) for i, j in places]
        spreads = [mean((block(i, j) - m) ** 2) for (i, j), m in zip(places, middles)]
        scales = [1.0 / jnp.sqrt(v + 1e-06) for v in spreads]
        for i in range(grid):
            highs, lows = [], []
            for j in range(grid):
                at = i * grid + j
                high, low = split((block(i, j) - middles[at]) * scales[at])
                highs.append(high)
                lows.append(low)
            stacked = jnp.concatenate(
                [jnp.concatenate(highs, 1), jnp.concatenate(lows, 1)], 0)
            seg = dot(first[:4 * ROWS], stacked)
            seg = seg[:2 * ROWS] + seg[2 * ROWS:]
            for j in range(grid):
                at = pl.ds((i * grid + j) * ROWS, ROWS)
                part = seg[:, j * PATCH:(j + 1) * PATCH]
                high, low = split(jnp.concatenate([part[:ROWS], part[ROWS:]], 1))
                seg_h[at] = high
                seg_l[at] = low
        high = seg_h[...]
        into[...] = dot(jnp.concatenate([high, seg_l[...], high], 1), second[...])

    def correlate(slot):
        a_r, a_i = spectra[0, :, :PATCH], spectra[0, :, PATCH:]
        b_r, b_i = spectra[1, :, :PATCH], spectra[1, :, PATCH:]
        high, low = split(jnp.concatenate([a_r * b_r + a_i * b_i, a_r * b_i - a_i * b_r], 1))
        half = dot(jnp.concatenate([high, low, high], 1), third[...])
        highs, lows = [], []
        for p in range(grid * grid):
            part = half[p * ROWS:(p + 1) * ROWS]
            high, low = split(jnp.concatenate([part[:, :PATCH], part[:, PATCH:]], 0))
            highs.append(high)
            lows.append(low)
        table = first[4 * ROWS:, :2 * ROWS]
        done = dot(table, jnp.concatenate(highs, 1))
        done = done[:CROP] + done[CROP:] + dot(table[:CROP], jnp.concatenate(lows, 1))
        for p in range(grid * grid):
            lined[pl.ds(p * CROP, CROP)] = done[:, p * PATCH:(p + 1) * PATCH]
        lane = lax.broadcasted_iota(jnp.int32, (grid * grid, PATCH), 1) // CROP
        per = PATCH // CROP
        listed = partners[0, slot] == 1
        for g in range(CROP // per):
            line = lined[pl.ds(g * per, grid * grid, stride=CROP)]
            for q in range(1, per):
                line = jnp.where(lane == q, lined[pl.ds(g * per + q, grid * grid, stride=CROP)], line)
            out_ref[pl.ds(slot * lines + g, grid * grid, stride=CROP // per)] = jnp.where(listed, line, 0.0)

    for load in loads:
        load.wait()

    def turn(step, carry):
        turned = jnp.where(odd & quick, lax.rem(step + 1, REACH), step - 1)
        slot = jnp.where(step == 0, REACH, turned)
        here = (step == 0) | (me + slot + 1 < total)

        @pl.when(step == 1)
        def _():
            start([(odd & sends[0][0],) + sends[0][1:]])

        @pl.when(step == 2)
        def _():
            start([(jnp.logical_not(quick) & sends[1][0],) + sends[1][1:]])

        @pl.when(here & (step > 0))
        def _():
            for c in range(CHUNKS):
                arrived(c, slot)

                @pl.when(slot == 1)
                def _():
                    forward_copy(c, jnp.where(even, 0, 2)).start()

        @pl.when(here)
        def _():
            transform(lambda r, c: slots[slot, r, c], spectra.at[jnp.minimum(step, 1)])

        @pl.when(here & (step > 0))
        def _():
            correlate(slot)

        @pl.when(jnp.logical_not(here))
        def _():
            out_ref[pl.ds(pl.multiple_of(slot * lines, 8), lines)] = jnp.zeros((lines, PATCH), jnp.float32)
        return carry

    lax.fori_loop(0, REACH + 1, turn, 0)

    for c in range(CHUNKS):
        for wanted, slot, device, which in sends:
            @pl.when(wanted)
            def _():
                send(c, slot, device, which).wait_send()

        @pl.when(me + 2 < total)
        def _():
            forward_copy(c, 0).wait_send()


def body(tiles, partners):
    side = tiles.shape[-1]
    grid = side // HALF - 1
    total = lax.axis_size("section")
    count = grid * grid
    lines = count * CROP * CROP // PATCH
    constants = tables()
    vmem = pl.BlockSpec(memory_space=pltpu.VMEM)
    result = pl.pallas_call(
        functools.partial(kernel, total, grid),
        out_shape=jax.ShapeDtypeStruct((REACH * lines, PATCH), jnp.float32),
        in_specs=[pl.BlockSpec(memory_space=pltpu.HBM)] * 5,
        out_specs=vmem,
        scratch_shapes=[
            pltpu.SMEM((1, REACH), jnp.int32),
            *[pltpu.VMEM(t.shape, BF) for t in constants],
            pltpu.SemaphoreType.DMA((5,)),
            pltpu.VMEM((REACH + 1, side, side), jnp.float32),
            pltpu.VMEM((2, count * ROWS, 2 * PATCH), jnp.float32),
            pltpu.VMEM((count * ROWS, 2 * PATCH), BF),
            pltpu.VMEM((count * ROWS, 2 * PATCH), BF),
            pltpu.VMEM((count * CROP, PATCH), jnp.float32),
            pltpu.SemaphoreType.DMA((2, CHUNKS)),
            pltpu.SemaphoreType.DMA((REACH, CHUNKS)),
            pltpu.SemaphoreType.DMA((CHUNKS,)),
        ],
        compiler_params=pltpu.CompilerParams(
            collective_id=0, has_side_effects=True, vmem_limit_bytes=63_000_000
        ),
    )(tiles[0], partners, *[jnp.asarray(t) for t in constants])
    result = lax.optimization_barrier(result * (1.0 / PATCH))
    return result.reshape(1, REACH, count, CROP * CROP)


def solution(mesh):
    in_specs = (P(("groups", "section"), None, None), P(("groups", "section"), None))
    out_specs = P(("groups", "section"), None, None, None)
    return jax.shard_map(body, mesh=mesh, in_specs=in_specs, out_specs=out_specs, check_vma=False)
```

```python
import functools
import math

import jax
import jax.numpy as jnp
import ml_dtypes
import numpy as np
from jax import lax
from jax.experimental import pallas as pl
from jax.experimental.pallas import tpu as pltpu
from jax.sharding import PartitionSpec as P

PATCH = 128
REACH = 3
CROP = 32
HALF = PATCH // 2
ROWS = 80
CHUNKS = 2
BF = jnp.bfloat16


def split_table(table):
    high = table.astype(ml_dtypes.bfloat16)
    low = (table - high.astype(np.float64)).astype(ml_dtypes.bfloat16)
    return high, low


def thrice(table):
    high, low = split_table(table)
    return np.concatenate([high, high, low], 0)


def tables():
    x = np.arange(PATCH)
    k = np.arange(ROWS)
    live = (k <= HALF)[:, None]
    turn = 2.0 * math.pi / PATCH
    angle = (k[:, None] * x[None, :] % PATCH) * turn
    column = np.concatenate([np.cos(angle) * live, np.sin(angle) * live], 0)
    high, low = split_table(column)
    first = np.concatenate(
        [np.concatenate([high, high], 1), np.concatenate([low, np.zeros_like(low)], 1)], 0
    )
    angle = (x[:, None] * x[None, :] % PATCH) * turn
    cosine, sine = np.cos(angle), np.sin(angle)
    second = thrice(np.block([[cosine, -sine], [-sine, -cosine]]))
    kept = np.arange(CROP) - CROP // 2
    angle = (x[:, None] * np.tile(kept, PATCH // CROP)[None, :] % PATCH) * turn
    cosine, sine = np.cos(angle), np.sin(angle)
    third = thrice(np.block([[cosine, sine], [-sine, cosine]]))
    weight = np.where(k == 0, 1.0, np.where(k < HALF, 2.0, np.where(k == HALF, 1.0, 0.0)))
    angle = (kept[:, None] * k[None, :] % PATCH) * turn
    last = np.concatenate([np.cos(angle) * weight, -np.sin(angle) * weight], 1) / float(PATCH**2)
    fourth = np.concatenate(split_table(last), 0)
    fourth = np.pad(fourth, ((0, 0), (0, first.shape[1] - fourth.shape[1])))
    return np.concatenate([first, fourth], 0), second, third


def split(value):
    high = value.astype(BF)
    return high, (value - high.astype(jnp.float32)).astype(BF)


def dot(a, b):
    return jnp.dot(a, b, preferred_element_type=jnp.float32)


def kernel(total, grid, tile_ref, partners_ref, first_ref, second_ref, third_ref, out_ref,
           partners, first, second, third, load_sem, slots, spectra, seg_h, seg_l, lined, send_sem, recv_sem, forward_sem):
    me = lax.axis_index("section")
    even = lax.rem(me, 2) == 0
    odd = jnp.logical_not(even)
    piece = tile_ref.shape[0] // CHUNKS
    partner = jnp.where(even, me + 1, me - 1)
    lines = out_ref.shape[0] // REACH

    loads = [
        pltpu.make_async_copy(source, into, load_sem.at[n])
        for n, (source, into) in enumerate([
            (tile_ref, slots.at[REACH]), (first_ref, first), (second_ref, second),
            (third_ref, third), (partners_ref, partners)])
    ]
    for load in loads:
        load.start()

    barrier = pltpu.get_barrier_semaphore()
    writers = [
        (me + 2 < total, me + 2),
        (even & (me + 1 < total), me + 1),
        (odd & (me + 3 < total), me + 3),
        (odd & (me + 1 < total), me - 1),
    ]
    targets = [
        me >= 2,
        even & (me >= 3),
        odd,
        even & (me + 2 < total),
    ]
    for wanted, device in writers:
        @pl.when(wanted)
        def _():
            pl.semaphore_signal(barrier, inc=1, device_id={"section": device},
                                device_id_type=pl.DeviceIdType.MESH)
    pl.semaphore_wait(barrier, sum(t.astype(jnp.int32) for t in targets))

    def rows(c):
        return pl.ds(c * piece, piece)

    def send(c, slot, device, which):
        return pltpu.make_async_remote_copy(
            src_ref=tile_ref.at[rows(c)], dst_ref=slots.at[slot, rows(c)],
            send_sem=send_sem.at[which, c], recv_sem=recv_sem.at[slot, c],
            device_id={"section": device}, device_id_type=pl.DeviceIdType.MESH)

    def forward_copy(c, slot):
        return pltpu.make_async_remote_copy(
            src_ref=slots.at[1, rows(c)], dst_ref=slots.at[slot, rows(c)],
            send_sem=forward_sem.at[c], recv_sem=recv_sem.at[slot, c],
            device_id={"section": partner}, device_id_type=pl.DeviceIdType.MESH)

    def arrived(c, slot):
        pltpu.make_async_remote_copy(
            src_ref=tile_ref.at[rows(c)], dst_ref=slots.at[slot, rows(c)],
            send_sem=send_sem.at[0, c], recv_sem=recv_sem.at[slot, c],
            device_id={"section": partner}, device_id_type=pl.DeviceIdType.MESH).wait_recv()

    sends = [(me >= 2, 1, me - 2, 0), (even & (me >= 3), 2, me - 3, 1), (odd, 0, me - 1, 1)]
    quick = lax.rem(me // 2, 2) == 1

    def start(which_sends):
        for c in range(CHUNKS):
            for wanted, slot, device, which in which_sends:
                @pl.when(wanted)
                def _():
                    send(c, slot, device, which).start()

    start([sends[0], sends[2], (quick & sends[1][0],) + sends[1][1:]])

    def transform(read, into):
        def block(i, j):
            return read(pl.ds(i * HALF, PATCH), pl.ds(j * HALF, PATCH))

        def mean(value):
            return jnp.sum(jnp.sum(value, 0, keepdims=True), 1, keepdims=True) * (1.0 / PATCH**2)

        places = [(i, j) for i in range(grid) for j in range(grid)]
        middles = [mean(block(i, j)) for i, j in places]
        spreads = [mean((block(i, j) - m) ** 2) for (i, j), m in zip(places, middles)]
        scales = [1.0 / jnp.sqrt(v + 1e-06) for v in spreads]
        for i in range(grid):
            highs, lows = [], []
            for j in range(grid):
                at = i * grid + j
                high, low = split((block(i, j) - middles[at]) * scales[at])
                highs.append(high)
                lows.append(low)
            stacked = jnp.concatenate(
                [jnp.concatenate(highs, 1), jnp.concatenate(lows, 1)], 0)
            seg = dot(first[:4 * ROWS], stacked)
            seg = seg[:2 * ROWS] + seg[2 * ROWS:]
            for j in range(grid):
                at = pl.ds((i * grid + j) * ROWS, ROWS)
                part = seg[:, j * PATCH:(j + 1) * PATCH]
                high, low = split(jnp.concatenate([part[:ROWS], part[ROWS:]], 1))
                seg_h[at] = high
                seg_l[at] = low
        high = seg_h[...]
        into[...] = dot(jnp.concatenate([high, seg_l[...], high], 1), second[...])

    def correlate(slot):
        a_r, a_i = spectra[0, :, :PATCH], spectra[0, :, PATCH:]
        b_r, b_i = spectra[1, :, :PATCH], spectra[1, :, PATCH:]
        high, low = split(jnp.concatenate([a_r * b_r + a_i * b_i, a_r * b_i - a_i * b_r], 1))
        half = dot(jnp.concatenate([high, low, high], 1), third[...])
        highs, lows = [], []
        for p in range(grid * grid):
            part = half[p * ROWS:(p + 1) * ROWS]
            high, low = split(jnp.concatenate([part[:, :PATCH], part[:, PATCH:]], 0))
            highs.append(high)
            lows.append(low)
        table = first[4 * ROWS:, :2 * ROWS]
        done = dot(table, jnp.concatenate(highs, 1))
        done = done[:CROP] + done[CROP:] + dot(table[:CROP], jnp.concatenate(lows, 1))
        for p in range(grid * grid):
            lined[pl.ds(p * CROP, CROP)] = done[:, p * PATCH:(p + 1) * PATCH]
        lane = lax.broadcasted_iota(jnp.int32, (grid * grid, PATCH), 1) // CROP
        per = PATCH // CROP
        listed = partners[0, slot] == 1
        for g in range(CROP // per):
            line = lined[pl.ds(g * per, grid * grid, stride=CROP)]
            for q in range(1, per):
                line = jnp.where(lane == q, lined[pl.ds(g * per + q, grid * grid, stride=CROP)], line)
            out_ref[pl.ds(slot * lines + g, grid * grid, stride=CROP // per)] = jnp.where(listed, line, 0.0)

    for load in loads:
        load.wait()

    def turn(step, carry):
        odd_slot = jnp.where(quick, REACH - step, jnp.where(step == REACH, 2, 2 - step))
        slot = jnp.where(step == 0, REACH, jnp.where(even, step - 1, odd_slot))
        here = (step == 0) | (me + slot + 1 < total)

        @pl.when(step == 2)
        def _():
            start([(jnp.logical_not(quick) & sends[1][0],) + sends[1][1:]])

        @pl.when(here & (step > 0))
        def _():
            for c in range(CHUNKS):
                arrived(c, slot)

                @pl.when(slot == 1)
                def _():
                    forward_copy(c, jnp.where(even, 0, 2)).start()

        @pl.when(here)
        def _():
            transform(lambda r, c: slots[slot, r, c], spectra.at[jnp.minimum(step, 1)])

        @pl.when(here & (step > 0))
        def _():
            correlate(slot)

        @pl.when(jnp.logical_not(here))
        def _():
            out_ref[pl.ds(pl.multiple_of(slot * lines, 8), lines)] = jnp.zeros((lines, PATCH), jnp.float32)
        return carry

    lax.fori_loop(0, REACH + 1, turn, 0)

    for c in range(CHUNKS):
        for wanted, slot, device, which in sends:
            @pl.when(wanted)
            def _():
                send(c, slot, device, which).wait_send()

        @pl.when(me + 2 < total)
        def _():
            forward_copy(c, 0).wait_send()


def body(tiles, partners):
    side = tiles.shape[-1]
    grid = side // HALF - 1
    total = lax.axis_size("section")
    count = grid * grid
    lines = count * CROP * CROP // PATCH
    constants = tables()
    vmem = pl.BlockSpec(memory_space=pltpu.VMEM)
    result = pl.pallas_call(
        functools.partial(kernel, total, grid),
        out_shape=jax.ShapeDtypeStruct((REACH * lines, PATCH), jnp.float32),
        in_specs=[pl.BlockSpec(memory_space=pltpu.HBM)] * 5,
        out_specs=vmem,
        scratch_shapes=[
            pltpu.SMEM((1, REACH), jnp.int32),
            *[pltpu.VMEM(t.shape, BF) for t in constants],
            pltpu.SemaphoreType.DMA((5,)),
            pltpu.VMEM((REACH + 1, side, side), jnp.float32),
            pltpu.VMEM((2, count * ROWS, 2 * PATCH), jnp.float32),
            pltpu.VMEM((count * ROWS, 2 * PATCH), BF),
            pltpu.VMEM((count * ROWS, 2 * PATCH), BF),
            pltpu.VMEM((count * CROP, PATCH), jnp.float32),
            pltpu.SemaphoreType.DMA((2, CHUNKS)),
            pltpu.SemaphoreType.DMA((REACH, CHUNKS)),
            pltpu.SemaphoreType.DMA((CHUNKS,)),
        ],
        compiler_params=pltpu.CompilerParams(
            collective_id=0, has_side_effects=True, vmem_limit_bytes=63_000_000
        ),
    )(tiles[0], partners, *[jnp.asarray(t) for t in constants])
    result = lax.optimization_barrier(result * (1.0 / PATCH))
    return result.reshape(1, REACH, count, CROP * CROP)


def solution(mesh):
    in_specs = (P(("groups", "section"), None, None), P(("groups", "section"), None))
    out_specs = P(("groups", "section"), None, None, None)
    return jax.shard_map(body, mesh=mesh, in_specs=in_specs, out_specs=out_specs, check_vma=False)
```

```python
import functools
import math

import jax
import jax.numpy as jnp
import ml_dtypes
import numpy as np
from jax import lax
from jax.experimental import pallas as pl
from jax.experimental.pallas import tpu as pltpu
from jax.sharding import PartitionSpec as P

PATCH = 128
REACH = 3
CROP = 32
HALF = PATCH // 2
ROWS = 80
CHUNKS = 2
BF = jnp.bfloat16


def split_table(table):
    high = table.astype(ml_dtypes.bfloat16)
    low = (table - high.astype(np.float64)).astype(ml_dtypes.bfloat16)
    return high, low


def thrice(table):
    high, low = split_table(table)
    return np.concatenate([high, high, low], 0)


def tables():
    x = np.arange(PATCH)
    k = np.arange(ROWS)
    live = (k <= HALF)[:, None]
    turn = 2.0 * math.pi / PATCH
    angle = (k[:, None] * x[None, :] % PATCH) * turn
    column = np.concatenate([np.cos(angle) * live, np.sin(angle) * live], 0)
    high, low = split_table(column)
    first = np.concatenate(
        [np.concatenate([high, high], 1), np.concatenate([low, np.zeros_like(low)], 1)], 0
    )
    angle = (x[:, None] * x[None, :] % PATCH) * turn
    cosine, sine = np.cos(angle), np.sin(angle)
    second = thrice(np.block([[cosine, -sine], [-sine, -cosine]]))
    kept = np.arange(CROP) - CROP // 2
    angle = (x[:, None] * np.tile(kept, PATCH // CROP)[None, :] % PATCH) * turn
    cosine, sine = np.cos(angle), np.sin(angle)
    third = thrice(np.block([[cosine, sine], [-sine, cosine]]))
    weight = np.where(k == 0, 1.0, np.where(k < HALF, 2.0, np.where(k == HALF, 1.0, 0.0)))
    angle = (kept[:, None] * k[None, :] % PATCH) * turn
    last = np.concatenate([np.cos(angle) * weight, -np.sin(angle) * weight], 1) / float(PATCH**2)
    fourth = np.concatenate(split_table(last), 0)
    fourth = np.pad(fourth, ((0, 0), (0, first.shape[1] - fourth.shape[1])))
    return np.concatenate([first, fourth], 0), second, third


def split(value):
    high = value.astype(BF)
    return high, (value - high.astype(jnp.float32)).astype(BF)


def dot(a, b):
    return jnp.dot(a, b, preferred_element_type=jnp.float32)


def kernel(total, grid, tile_ref, partners_ref, first_ref, second_ref, third_ref, result_ref,
           out_ref, store_sem,
           partners, first, second, third, load_sem, slots, spectra, seg_h, seg_l, lined, send_sem, recv_sem, forward_sem):
    me = lax.axis_index("section")
    even = lax.rem(me, 2) == 0
    odd = jnp.logical_not(even)
    piece = tile_ref.shape[0] // CHUNKS
    partner = jnp.where(even, me + 1, me - 1)
    lines = out_ref.shape[0] // REACH

    loads = [
        pltpu.make_async_copy(source, into, load_sem.at[n])
        for n, (source, into) in enumerate([
            (tile_ref, slots.at[REACH]), (first_ref, first), (second_ref, second),
            (third_ref, third), (partners_ref, partners)])
    ]
    for load in loads:
        load.start()

    barrier = pltpu.get_barrier_semaphore()
    writers = [
        (me + 2 < total, me + 2),
        (even & (me + 1 < total), me + 1),
        (odd & (me + 3 < total), me + 3),
        (odd & (me + 1 < total), me - 1),
    ]
    targets = [
        me >= 2,
        even & (me >= 3),
        odd,
        even & (me + 2 < total),
    ]
    for wanted, device in writers:
        @pl.when(wanted)
        def _():
            pl.semaphore_signal(barrier, inc=1, device_id={"section": device},
                                device_id_type=pl.DeviceIdType.MESH)
    pl.semaphore_wait(barrier, sum(t.astype(jnp.int32) for t in targets))

    def rows(c):
        return pl.ds(c * piece, piece)

    def send(c, slot, device, which):
        return pltpu.make_async_remote_copy(
            src_ref=tile_ref.at[rows(c)], dst_ref=slots.at[slot, rows(c)],
            send_sem=send_sem.at[which, c], recv_sem=recv_sem.at[slot, c],
            device_id={"section": device}, device_id_type=pl.DeviceIdType.MESH)

    def forward_copy(c, slot):
        return pltpu.make_async_remote_copy(
            src_ref=slots.at[1, rows(c)], dst_ref=slots.at[slot, rows(c)],
            send_sem=forward_sem.at[c], recv_sem=recv_sem.at[slot, c],
            device_id={"section": partner}, device_id_type=pl.DeviceIdType.MESH)

    def arrived(c, slot):
        pltpu.make_async_remote_copy(
            src_ref=tile_ref.at[rows(c)], dst_ref=slots.at[slot, rows(c)],
            send_sem=send_sem.at[0, c], recv_sem=recv_sem.at[slot, c],
            device_id={"section": partner}, device_id_type=pl.DeviceIdType.MESH).wait_recv()

    sends = [(me >= 2, 1, me - 2, 0), (even & (me >= 3), 2, me - 3, 1), (odd, 0, me - 1, 1)]
    quick = lax.rem(me // 2, 2) == 1

    def start(which_sends):
        for c in range(CHUNKS):
            for wanted, slot, device, which in which_sends:
                @pl.when(wanted)
                def _():
                    send(c, slot, device, which).start()

    start([sends[0], sends[2], (quick & sends[1][0],) + sends[1][1:]])

    def transform(read, into):
        def block(i, j):
            return read(pl.ds(i * HALF, PATCH), pl.ds(j * HALF, PATCH))

        def mean(value):
            return jnp.sum(jnp.sum(value, 0, keepdims=True), 1, keepdims=True) * (1.0 / PATCH**2)

        places = [(i, j) for i in range(grid) for j in range(grid)]
        middles = [mean(block(i, j)) for i, j in places]
        spreads = [mean((block(i, j) - m) ** 2) for (i, j), m in zip(places, middles)]
        scales = [1.0 / jnp.sqrt(v + 1e-06) for v in spreads]
        for i in range(grid):
            highs, lows = [], []
            for j in range(grid):
                at = i * grid + j
                high, low = split((block(i, j) - middles[at]) * scales[at])
                highs.append(high)
                lows.append(low)
            stacked = jnp.concatenate(
                [jnp.concatenate(highs, 1), jnp.concatenate(lows, 1)], 0)
            seg = dot(first[:4 * ROWS], stacked)
            seg = seg[:2 * ROWS] + seg[2 * ROWS:]
            for j in range(grid):
                at = pl.ds((i * grid + j) * ROWS, ROWS)
                part = seg[:, j * PATCH:(j + 1) * PATCH]
                high, low = split(jnp.concatenate([part[:ROWS], part[ROWS:]], 1))
                seg_h[at] = high
                seg_l[at] = low
        high = seg_h[...]
        into[...] = dot(jnp.concatenate([high, seg_l[...], high], 1), second[...])

    def correlate(slot):
        a_r, a_i = spectra[0, :, :PATCH], spectra[0, :, PATCH:]
        b_r, b_i = spectra[1, :, :PATCH], spectra[1, :, PATCH:]
        high, low = split(jnp.concatenate([a_r * b_r + a_i * b_i, a_r * b_i - a_i * b_r], 1))
        half = dot(jnp.concatenate([high, low, high], 1), third[...])
        highs, lows = [], []
        for p in range(grid * grid):
            part = half[p * ROWS:(p + 1) * ROWS]
            high, low = split(jnp.concatenate([part[:, :PATCH], part[:, PATCH:]], 0))
            highs.append(high)
            lows.append(low)
        table = first[4 * ROWS:, :2 * ROWS]
        done = dot(table, jnp.concatenate(highs, 1))
        done = done[:CROP] + done[CROP:] + dot(table[:CROP], jnp.concatenate(lows, 1))
        for p in range(grid * grid):
            lined[pl.ds(p * CROP, CROP)] = done[:, p * PATCH:(p + 1) * PATCH]
        lane = lax.broadcasted_iota(jnp.int32, (grid * grid, PATCH), 1) // CROP
        per = PATCH // CROP
        listed = partners[0, slot] == 1
        for g in range(CROP // per):
            line = lined[pl.ds(g * per, grid * grid, stride=CROP)]
            for q in range(1, per):
                line = jnp.where(lane == q, lined[pl.ds(g * per + q, grid * grid, stride=CROP)], line)
            out_ref[pl.ds(slot * lines + g, grid * grid, stride=CROP // per)] = jnp.where(listed, line, 0.0)

    for load in loads[:3]:
        load.wait()

    def turn(step, carry):
        odd_slot = jnp.where(quick, REACH - step, jnp.where(step == REACH, 2, 2 - step))
        slot = jnp.where(step == 0, REACH, jnp.where(even, step - 1, odd_slot))
        here = (step == 0) | (me + slot + 1 < total)

        @pl.when(step == 1)
        def _():
            for load in loads[3:]:
                load.wait()

        @pl.when(step == 2)
        def _():
            start([(jnp.logical_not(quick) & sends[1][0],) + sends[1][1:]])

        @pl.when(here & (step > 0))
        def _():
            for c in range(CHUNKS):
                arrived(c, slot)

                @pl.when(slot == 1)
                def _():
                    forward_copy(c, jnp.where(even, 0, 2)).start()

        @pl.when(here)
        def _():
            transform(lambda r, c: slots[slot, r, c], spectra.at[jnp.minimum(step, 1)])

        @pl.when(here & (step > 0))
        def _():
            correlate(slot)

        @pl.when(jnp.logical_not(here))
        def _():
            out_ref[pl.ds(pl.multiple_of(slot * lines, 8), lines)] = jnp.zeros((lines, PATCH), jnp.float32)

        @pl.when(step > 0)
        def _():
            store(slot).start()
        return carry

    def store(slot):
        at = pl.ds(slot * lines, lines)
        return pltpu.make_async_copy(out_ref.at[at], result_ref.at[at], store_sem.at[slot])

    lax.fori_loop(0, REACH + 1, turn, 0)
    for slot in range(REACH):
        store(slot).wait()

    for c in range(CHUNKS):
        for wanted, slot, device, which in sends:
            @pl.when(wanted)
            def _():
                send(c, slot, device, which).wait_send()

        @pl.when(me + 2 < total)
        def _():
            forward_copy(c, 0).wait_send()


def body(tiles, partners):
    side = tiles.shape[-1]
    grid = side // HALF - 1
    total = lax.axis_size("section")
    count = grid * grid
    lines = count * CROP * CROP // PATCH
    constants = tables()
    result = pl.pallas_call(
        functools.partial(kernel, total, grid),
        out_shape=jax.ShapeDtypeStruct((REACH * lines, PATCH), jnp.float32),
        in_specs=[pl.BlockSpec(memory_space=pltpu.HBM)] * 5,
        out_specs=pl.BlockSpec(memory_space=pltpu.HBM),
        scratch_shapes=[
            pltpu.VMEM((REACH * lines, PATCH), jnp.float32),
            pltpu.SemaphoreType.DMA((REACH,)),
            pltpu.SMEM((1, REACH), jnp.int32),
            *[pltpu.VMEM(t.shape, BF) for t in constants],
            pltpu.SemaphoreType.DMA((5,)),
            pltpu.VMEM((REACH + 1, side, side), jnp.float32),
            pltpu.VMEM((2, count * ROWS, 2 * PATCH), jnp.float32),
            pltpu.VMEM((count * ROWS, 2 * PATCH), BF),
            pltpu.VMEM((count * ROWS, 2 * PATCH), BF),
            pltpu.VMEM((count * CROP, PATCH), jnp.float32),
            pltpu.SemaphoreType.DMA((2, CHUNKS)),
            pltpu.SemaphoreType.DMA((REACH, CHUNKS)),
            pltpu.SemaphoreType.DMA((CHUNKS,)),
        ],
        compiler_params=pltpu.CompilerParams(
            collective_id=0, has_side_effects=True, vmem_limit_bytes=63_000_000
        ),
    )(tiles[0], partners, *[jnp.asarray(t) for t in constants])
    result = lax.optimization_barrier(result * (1.0 / PATCH))
    return result.reshape(1, REACH, count, CROP * CROP)


def solution(mesh):
    in_specs = (P(("groups", "section"), None, None), P(("groups", "section"), None))
    out_specs = P(("groups", "section"), None, None, None)
    return jax.shard_map(body, mesh=mesh, in_specs=in_specs, out_specs=out_specs, check_vma=False)
```

```python
import functools
import math

import jax
import jax.numpy as jnp
import ml_dtypes
import numpy as np
from jax import lax
from jax.experimental import pallas as pl
from jax.experimental.pallas import tpu as pltpu
from jax.sharding import PartitionSpec as P

PATCH = 128
REACH = 3
CROP = 32
HALF = PATCH // 2
ROWS = 80
CHUNKS = 4
BF = jnp.bfloat16


def split_table(table):
    high = table.astype(ml_dtypes.bfloat16)
    low = (table - high.astype(np.float64)).astype(ml_dtypes.bfloat16)
    return high, low


def thrice(table):
    high, low = split_table(table)
    return np.concatenate([high, high, low], 0)


def tables():
    x = np.arange(PATCH)
    k = np.arange(ROWS)
    live = (k <= HALF)[:, None]
    turn = 2.0 * math.pi / PATCH
    angle = (k[:, None] * x[None, :] % PATCH) * turn
    column = np.concatenate([np.cos(angle) * live, np.sin(angle) * live], 0)
    high, low = split_table(column)
    first = np.concatenate(
        [np.concatenate([high, high], 1), np.concatenate([low, np.zeros_like(low)], 1)], 0
    )
    angle = (x[:, None] * x[None, :] % PATCH) * turn
    cosine, sine = np.cos(angle), np.sin(angle)
    second = thrice(np.block([[cosine, -sine], [-sine, -cosine]]))
    kept = np.arange(CROP) - CROP // 2
    angle = (x[:, None] * np.tile(kept, PATCH // CROP)[None, :] % PATCH) * turn
    cosine, sine = np.cos(angle), np.sin(angle)
    third = thrice(np.block([[cosine, sine], [-sine, cosine]]))
    weight = np.where(k == 0, 1.0, np.where(k < HALF, 2.0, np.where(k == HALF, 1.0, 0.0)))
    angle = (kept[:, None] * k[None, :] % PATCH) * turn
    last = np.concatenate([np.cos(angle) * weight, -np.sin(angle) * weight], 1) / float(PATCH**2)
    fourth = np.concatenate(split_table(last), 0)
    fourth = np.pad(fourth, ((0, 0), (0, first.shape[1] - fourth.shape[1])))
    return np.concatenate([first, fourth], 0), second, third


def split(value):
    high = value.astype(BF)
    return high, (value - high.astype(jnp.float32)).astype(BF)


def dot(a, b):
    return jnp.dot(a, b, preferred_element_type=jnp.float32)


def kernel(total, grid, tile_ref, partners_ref, first_ref, second_ref, third_ref, result_ref,
           out_ref, store_sem,
           partners, first, second, third, load_sem, slots, spectra, seg_h, seg_l, lined, send_sem, recv_sem, forward_sem):
    me = lax.axis_index("section")
    even = lax.rem(me, 2) == 0
    odd = jnp.logical_not(even)
    piece = tile_ref.shape[0] // CHUNKS
    partner = jnp.where(even, me + 1, me - 1)
    lines = out_ref.shape[0] // REACH

    loads = [
        pltpu.make_async_copy(source, into, load_sem.at[n])
        for n, (source, into) in enumerate([
            (tile_ref, slots.at[REACH]), (first_ref, first), (second_ref, second),
            (third_ref, third), (partners_ref, partners)])
    ]
    for load in loads:
        load.start()

    barrier = pltpu.get_barrier_semaphore()
    writers = [
        (me + 2 < total, me + 2),
        (even & (me + 1 < total), me + 1),
        (odd & (me + 3 < total), me + 3),
        (odd & (me + 1 < total), me - 1),
    ]
    targets = [
        me >= 2,
        even & (me >= 3),
        odd,
        even & (me + 2 < total),
    ]
    for wanted, device in writers:
        @pl.when(wanted)
        def _():
            pl.semaphore_signal(barrier, inc=1, device_id={"section": device},
                                device_id_type=pl.DeviceIdType.MESH)
    pl.semaphore_wait(barrier, sum(t.astype(jnp.int32) for t in targets))

    def rows(c):
        return pl.ds(c * piece, piece)

    def send(c, slot, device, which):
        return pltpu.make_async_remote_copy(
            src_ref=tile_ref.at[rows(c)], dst_ref=slots.at[slot, rows(c)],
            send_sem=send_sem.at[which, c], recv_sem=recv_sem.at[slot, c],
            device_id={"section": device}, device_id_type=pl.DeviceIdType.MESH)

    def forward_copy(c, slot):
        return pltpu.make_async_remote_copy(
            src_ref=slots.at[1, rows(c)], dst_ref=slots.at[slot, rows(c)],
            send_sem=forward_sem.at[c], recv_sem=recv_sem.at[slot, c],
            device_id={"section": partner}, device_id_type=pl.DeviceIdType.MESH)

    def arrived(c, slot):
        pltpu.make_async_remote_copy(
            src_ref=tile_ref.at[rows(c)], dst_ref=slots.at[slot, rows(c)],
            send_sem=send_sem.at[0, c], recv_sem=recv_sem.at[slot, c],
            device_id={"section": partner}, device_id_type=pl.DeviceIdType.MESH).wait_recv()

    sends = [(me >= 2, 1, me - 2, 0), (even & (me >= 3), 2, me - 3, 1), (odd, 0, me - 1, 1)]
    quick = lax.rem(me // 2, 2) == 1

    def start(which_sends):
        for c in range(CHUNKS):
            for wanted, slot, device, which in which_sends:
                @pl.when(wanted)
                def _():
                    send(c, slot, device, which).start()

    start([sends[0], sends[2], (quick & sends[1][0],) + sends[1][1:]])

    def transform(read, into):
        def block(i, j):
            return read(pl.ds(i * HALF, PATCH), pl.ds(j * HALF, PATCH))

        def mean(value):
            return jnp.sum(jnp.sum(value, 0, keepdims=True), 1, keepdims=True) * (1.0 / PATCH**2)

        places = [(i, j) for i in range(grid) for j in range(grid)]
        middles = [mean(block(i, j)) for i, j in places]
        spreads = [mean((block(i, j) - m) ** 2) for (i, j), m in zip(places, middles)]
        scales = [1.0 / jnp.sqrt(v + 1e-06) for v in spreads]
        for i in range(grid):
            highs, lows = [], []
            for j in range(grid):
                at = i * grid + j
                high, low = split((block(i, j) - middles[at]) * scales[at])
                highs.append(high)
                lows.append(low)
            stacked = jnp.concatenate(
                [jnp.concatenate(highs, 1), jnp.concatenate(lows, 1)], 0)
            seg = dot(first[:4 * ROWS], stacked)
            seg = seg[:2 * ROWS] + seg[2 * ROWS:]
            for j in range(grid):
                at = pl.ds((i * grid + j) * ROWS, ROWS)
                part = seg[:, j * PATCH:(j + 1) * PATCH]
                high, low = split(jnp.concatenate([part[:ROWS], part[ROWS:]], 1))
                seg_h[at] = high
                seg_l[at] = low
        high = seg_h[...]
        into[...] = dot(jnp.concatenate([high, seg_l[...], high], 1), second[...])

    def correlate(slot):
        a_r, a_i = spectra[0, :, :PATCH], spectra[0, :, PATCH:]
        b_r, b_i = spectra[1, :, :PATCH], spectra[1, :, PATCH:]
        high, low = split(jnp.concatenate([a_r * b_r + a_i * b_i, a_r * b_i - a_i * b_r], 1))
        half = dot(jnp.concatenate([high, low, high], 1), third[...])
        highs, lows = [], []
        for p in range(grid * grid):
            part = half[p * ROWS:(p + 1) * ROWS]
            high, low = split(jnp.concatenate([part[:, :PATCH], part[:, PATCH:]], 0))
            highs.append(high)
            lows.append(low)
        table = first[4 * ROWS:, :2 * ROWS]
        done = dot(table, jnp.concatenate(highs, 1))
        done = done[:CROP] + done[CROP:] + dot(table[:CROP], jnp.concatenate(lows, 1))
        for p in range(grid * grid):
            lined[pl.ds(p * CROP, CROP)] = done[:, p * PATCH:(p + 1) * PATCH]
        lane = lax.broadcasted_iota(jnp.int32, (grid * grid, PATCH), 1) // CROP
        per = PATCH // CROP
        listed = partners[0, slot] == 1
        for g in range(CROP // per):
            line = lined[pl.ds(g * per, grid * grid, stride=CROP)]
            for q in range(1, per):
                line = jnp.where(lane == q, lined[pl.ds(g * per + q, grid * grid, stride=CROP)], line)
            out_ref[pl.ds(slot * lines + g, grid * grid, stride=CROP // per)] = jnp.where(listed, line, 0.0)

    for load in loads[:3]:
        load.wait()

    def turn(step, carry):
        odd_slot = jnp.where(quick, REACH - step, jnp.where(step == REACH, 2, 2 - step))
        slot = jnp.where(step == 0, REACH, jnp.where(even, step - 1, odd_slot))
        here = (step == 0) | (me + slot + 1 < total)

        @pl.when(step == 1)
        def _():
            for load in loads[3:]:
                load.wait()

        @pl.when(step == 2)
        def _():
            start([(jnp.logical_not(quick) & sends[1][0],) + sends[1][1:]])

        @pl.when(here & (step > 0))
        def _():
            for c in range(CHUNKS):
                arrived(c, slot)

                @pl.when(slot == 1)
                def _():
                    forward_copy(c, jnp.where(even, 0, 2)).start()

        @pl.when(here)
        def _():
            transform(lambda r, c: slots[slot, r, c], spectra.at[jnp.minimum(step, 1)])

        @pl.when(here & (step > 0))
        def _():
            correlate(slot)

        @pl.when(jnp.logical_not(here))
        def _():
            out_ref[pl.ds(pl.multiple_of(slot * lines, 8), lines)] = jnp.zeros((lines, PATCH), jnp.float32)

        @pl.when(step > 0)
        def _():
            store(slot).start()
        return carry

    def store(slot):
        at = pl.ds(slot * lines, lines)
        return pltpu.make_async_copy(out_ref.at[at], result_ref.at[at], store_sem.at[slot])

    lax.fori_loop(0, REACH + 1, turn, 0)
    for slot in range(REACH):
        store(slot).wait()

    for c in range(CHUNKS):
        for wanted, slot, device, which in sends:
            @pl.when(wanted)
            def _():
                send(c, slot, device, which).wait_send()

        @pl.when(me + 2 < total)
        def _():
            forward_copy(c, 0).wait_send()


def body(tiles, partners):
    side = tiles.shape[-1]
    grid = side // HALF - 1
    total = lax.axis_size("section")
    count = grid * grid
    lines = count * CROP * CROP // PATCH
    constants = tables()
    result = pl.pallas_call(
        functools.partial(kernel, total, grid),
        out_shape=jax.ShapeDtypeStruct((REACH * lines, PATCH), jnp.float32),
        in_specs=[pl.BlockSpec(memory_space=pltpu.HBM)] * 5,
        out_specs=pl.BlockSpec(memory_space=pltpu.HBM),
        scratch_shapes=[
            pltpu.VMEM((REACH * lines, PATCH), jnp.float32),
            pltpu.SemaphoreType.DMA((REACH,)),
            pltpu.SMEM((1, REACH), jnp.int32),
            *[pltpu.VMEM(t.shape, BF) for t in constants],
            pltpu.SemaphoreType.DMA((5,)),
            pltpu.VMEM((REACH + 1, side, side), jnp.float32),
            pltpu.VMEM((2, count * ROWS, 2 * PATCH), jnp.float32),
            pltpu.VMEM((count * ROWS, 2 * PATCH), BF),
            pltpu.VMEM((count * ROWS, 2 * PATCH), BF),
            pltpu.VMEM((count * CROP, PATCH), jnp.float32),
            pltpu.SemaphoreType.DMA((2, CHUNKS)),
            pltpu.SemaphoreType.DMA((REACH, CHUNKS)),
            pltpu.SemaphoreType.DMA((CHUNKS,)),
        ],
        compiler_params=pltpu.CompilerParams(
            collective_id=0, has_side_effects=True, vmem_limit_bytes=63_000_000
        ),
    )(tiles[0], partners, *[jnp.asarray(t) for t in constants])
    result = lax.optimization_barrier(result * (1.0 / PATCH))
    return result.reshape(1, REACH, count, CROP * CROP)


def solution(mesh):
    in_specs = (P(("groups", "section"), None, None), P(("groups", "section"), None))
    out_specs = P(("groups", "section"), None, None, None)
    return jax.shard_map(body, mesh=mesh, in_specs=in_specs, out_specs=out_specs, check_vma=False)
```
